32 devices in a mesh: edges: 32 (over z, y, x, core).
Axes of the slice: x: 2, y: 2, z: 4, core: 2. Of those that a mesh axis runs over, the one named last changes fastest.
Arguments:
- messages: float32 [12288, 512], P('edges'), may hold values from -6 to 6
- rev_slot: int32 [12288], P('edges'), may hold values from 0 to 95, as said below
- tri_basis: float32 [16, 49152], P(None, 'edges'), may hold values from -6 to 6
- tri_source: int32 [49152], P('edges'), may hold values from 0 to 575
- tri_target: int32 [49152], P('edges'), may hold values from 0 to 127
- tile_block: int32 [384], P('edges'), may hold values from 0 to 2
- tile_count: int32 [32], P('edges'), may hold values from 6 to 12, as said below
- w_basis: float32 [16, 512], replicated, may hold values from -1.5 to 1.5
- w_rev: float32 [512, 512], replicated, may hold values from -0.25 to 0.25
- w_layers: float32 [2, 512, 512], replicated, may hold values from -0.25 to 0.25
- cotangent: float32 [12288, 512], P('edges'), may hold values from -6 to 6
Outputs:
- out_messages: float32 [12288, 512], P('edges')
- grad_messages: float32 [12288, 512], P('edges')
- grad_layers: float32 [2, 262144], P(None, 'edges')
- grad_rev: float32 [262144], P('edges')
- grad_basis: float32 [16, 512], replicated
The draws below stay inside these ranges and needn't reach their ends.
Inputs may be any that keep to these rules, and one draw needn't show every extreme that they name: rev_slot pairs every edge with a reverse edge as in the reference program, and the pairing is an involution: the reverse of an edge's reverse is the edge itself. Tiles j >= tile_count[d] of device d are ignored whatever they hold; some device has 12 live tiles.
All inputs are finite; a program needn't handle non-finite values.
Results may differ from the reference program's by a relative error of at most 0.0003.
Values sent between devices are 32-bit elements; how exact they have to be, the bound alone decides.
A program may use at most 64 MiB of HBM per device.

```python
import jax
import jax.numpy as jnp
import numpy as np
from jax import lax

D = 512
NB = 16
LAYERS = 2
E_DEV = 384
TILE_CAP = 12
HALO = 96
GROUP = 96
EDGES = 12288
TILES = 384
TRIPS = 49152
N_EDGES = 32


def draw_tile_count(key, part):
    counts = jax.random.randint(jax.random.fold_in(key, 11), (N_EDGES,), TILE_CAP // 2, TILE_CAP + 1)
    busiest = jax.random.randint(jax.random.fold_in(key, 12), (), 0, N_EDGES)
    return jnp.where(jnp.arange(N_EDGES) == busiest, TILE_CAP, counts).astype(jnp.int32)


def draw_rev_slot(key, part):
    levels = N_EDGES.bit_length() - 1
    bit_table = jnp.asarray(np.array([0, levels // 3, 2 * levels // 3, levels - 1], np.int32))
    base_key = jax.random.fold_in(key, 21)

    def one_group(device, group_id):
        bit_pos = bit_table[group_id]
        upper = jnp.bitwise_and(jnp.right_shift(device, bit_pos), 1)
        lower_dev = device - upper * jnp.left_shift(jnp.int32(1), bit_pos)
        order = jax.random.permutation(jax.random.fold_in(base_key, lower_dev * 4 + group_id), GROUP)
        inverse = jnp.argsort(order)
        return jnp.where(upper == 1, inverse, order)

    def one_device(device):
        return jax.vmap(lambda group_id: one_group(device, group_id))(jnp.arange(4, dtype=jnp.int32))
    table = jax.vmap(one_device)(jnp.arange(N_EDGES, dtype=jnp.int32))
    return table.reshape(N_EDGES * E_DEV).astype(jnp.int32)


def touch_ends(drawn, stream_key, least, top_value):
    extent = drawn.shape
    place = [jax.random.randint(jax.random.fold_in(stream_key, axis), (), 0, extent[axis]) for axis in range(len(extent))]
    drawn = drawn.at[tuple(place)].set(least)
    longest = extent.index(max(extent))
    place[longest] = (place[longest] + 1) % extent[longest]
    return drawn.at[tuple(place)].set(top_value)


def block_levels(own_key, shape, shards, low, top_value):
    level, own = 1.0, jax.random.fold_in(own_key, 6)
    for position, parts in shards:
        draws = jnp.exp(jax.random.uniform(jax.random.fold_in(own, position), (parts,), jnp.float32, low / len(shards), top_value / len(shards)))
        level = level * jnp.repeat(draws, shape[position] // parts).reshape([-1 if axis == position else 1 for axis in range(len(shape))])
    return level


def centred(rng, extent, spread, bound, split=(), held_as=jnp.bfloat16):
    level = block_levels(rng, extent, split, -0.22, 0.18) if split else 1.0
    values = jax.random.normal(rng, extent, jnp.float32) * spread * level
    return jnp.minimum(jnp.maximum(values, -bound), bound).astype(held_as)


def setup_inputs(seed: int = 0) -> dict:
    key_list = jax.random.split(jax.random.key(seed), 12)
    return {
        "messages": centred(key_list[0], (EDGES, D), 1.0, 6.0, ((0, 32),), jnp.float32),
        "rev_slot": draw_rev_slot(jax.random.fold_in(key_list[11], 71), 0),
        "tri_basis": centred(key_list[2], (NB, TRIPS), 1.0, 6.0, ((1, 32),), jnp.float32),
        "tri_source": touch_ends(jax.random.randint(key_list[3], (TRIPS,), 0, E_DEV + 2 * HALO), jax.random.fold_in(key_list[3], 1), 0, (E_DEV + 2 * HALO) - 1).astype(jnp.int32),
        "tri_target": touch_ends(jax.random.randint(key_list[4], (TRIPS,), 0, 128), jax.random.fold_in(key_list[4], 1), 0, 127).astype(jnp.int32),
        "tile_block": touch_ends(jax.random.randint(key_list[5], (TILES,), 0, E_DEV // 128), jax.random.fold_in(key_list[5], 1), 0, (E_DEV // 128) - 1).astype(jnp.int32),
        "tile_count": draw_tile_count(jax.random.fold_in(key_list[11], 71), 0),
        "w_basis": centred(key_list[7], (NB, D), NB ** -0.5, 1.5, (), jnp.float32),
        "w_rev": centred(key_list[8], (D, D), D ** -0.5, 0.25, (), jnp.float32),
        "w_layers": centred(key_list[9], (LAYERS, D, D), D ** -0.5, 0.25, (), jnp.float32),
        "cotangent": centred(key_list[10], (EDGES, D), 1.0, 6.0, ((0, 32),), jnp.float32),
    }


def full_dot(left, right):
    return jnp.dot(left, right, precision=lax.Precision.HIGHEST, preferred_element_type=jnp.float32)


def lead_dot(left, right):
    return lax.dot_general(left, right, (((0,), (0,)), ((), ())), precision=lax.Precision.HIGHEST, preferred_element_type=jnp.float32)


def trail_dot(left, right):
    return lax.dot_general(left, right, (((1,), (1,)), ((), ())), precision=lax.Precision.HIGHEST, preferred_element_type=jnp.float32)


def silu_slope(values):
    sigma = jax.nn.sigmoid(values)
    return sigma * (1.0 + values * (1.0 - sigma))


def partner_index(rev_slot):
    levels = N_EDGES.bit_length() - 1
    bit_table = jnp.asarray(np.array([0, levels // 3, 2 * levels // 3, levels - 1], np.int32))
    flat = jnp.arange(N_EDGES * E_DEV, dtype=jnp.int32)
    device = flat // E_DEV
    group_id = (flat % E_DEV) // GROUP
    partner = jnp.bitwise_xor(device, jnp.left_shift(jnp.int32(1), bit_table[group_id]))
    return (partner * E_DEV + group_id * GROUP + rev_slot).astype(jnp.int32)


def reference(messages, rev_slot, tri_basis, tri_source, tri_target, tile_block, tile_count, w_basis, w_rev, w_layers, cotangent):
    slots = TILE_CAP * 128
    scale = float(EDGES) ** -0.5
    stacked = messages.reshape(N_EDGES, E_DEV, D)
    partner = partner_index(rev_slot)
    rev_msg = jnp.take(messages, partner, axis=0)
    rev_proj = full_dot(rev_msg, w_rev)
    gate_vals = jax.nn.silu(rev_proj)

    def device_tiles(device):
        before = lax.dynamic_index_in_dim(stacked, (device + N_EDGES - 1) % N_EDGES, 0, keepdims=False)
        own = lax.dynamic_index_in_dim(stacked, device, 0, keepdims=False)
        after = lax.dynamic_index_in_dim(stacked, (device + 1) % N_EDGES, 0, keepdims=False)
        window = jnp.concatenate([before[E_DEV - HALO:], own, after[:HALO]], axis=0)
        source = lax.dynamic_slice_in_dim(tri_source, device * slots, slots)
        target = lax.dynamic_slice_in_dim(tri_target, device * slots, slots)
        blocks = lax.dynamic_slice_in_dim(tile_block, device * TILE_CAP, TILE_CAP)
        coeffs = lax.dynamic_slice_in_dim(tri_basis, device * slots, slots, 1)
        live_tiles = (jnp.arange(TILE_CAP, dtype=jnp.int32) < tile_count[device]).astype(jnp.float32)
        live = jnp.repeat(live_tiles, 128)
        edge_row = (jnp.repeat(blocks, 128) * 128 + target).astype(jnp.int32)
        gathered = jnp.take(window, source, axis=0)
        tri_weight = lead_dot(coeffs, w_basis)
        return source, edge_row, live, gathered, tri_weight, coeffs

    def forward_agg(device):
        source, edge_row, live, gathered, tri_weight, coeffs = device_tiles(device)
        terms = gathered * tri_weight * live[:, None]
        return jax.ops.segment_sum(terms, edge_row, num_segments=E_DEV)

    devices = jnp.arange(N_EDGES, dtype=jnp.int32)
    agg = lax.map(forward_agg, devices).reshape(N_EDGES * E_DEV, D)
    hidden = messages + agg + messages * gate_vals
    states = [hidden]
    pre_list = []
    for layer in range(LAYERS):
        pre_act = full_dot(hidden, w_layers[layer])
        pre_list.append(pre_act)
        hidden = hidden + jax.nn.silu(pre_act)
        states.append(hidden)
    out_messages = hidden

    grad = cotangent
    layer_grads = [None] * LAYERS
    for layer in range(LAYERS - 1, -1, -1):
        grad_pre = grad * silu_slope(pre_list[layer])
        layer_grads[layer] = (lead_dot(states[layer], grad_pre) * scale).reshape(D * D)
        grad = grad + trail_dot(grad_pre, w_layers[layer])
    grad_agg = grad
    grad_msg = grad * (1.0 + gate_vals)
    grad_rev_proj = grad * messages * silu_slope(rev_proj)
    grad_rev = (lead_dot(rev_msg, grad_rev_proj) * scale).reshape(D * D)
    grad_rows = trail_dot(grad_rev_proj, w_rev)
    grad_msg = grad_msg + jnp.take(grad_rows, partner, axis=0)
    grad_stack = grad_agg.reshape(N_EDGES, E_DEV, D)

    def backward_tiles(device):
        source, edge_row, live, gathered, tri_weight, coeffs = device_tiles(device)
        own_grad = lax.dynamic_index_in_dim(grad_stack, device, 0, keepdims=False)
        grad_prod = jnp.take(own_grad, edge_row, axis=0) * live[:, None]
        window_grad = jax.ops.segment_sum(grad_prod * tri_weight, source, num_segments=E_DEV + 2 * HALO)
        basis_part = full_dot(coeffs, grad_prod * gathered)
        return window_grad, basis_part

    window_grads, basis_parts = lax.map(backward_tiles, devices)
    result = grad_msg.reshape(N_EDGES, E_DEV, D) + window_grads[:, HALO:HALO + E_DEV]
    result = result.at[:, E_DEV - HALO:].add(jnp.roll(window_grads[:, :HALO], -1, axis=0))
    result = result.at[:, :HALO].add(jnp.roll(window_grads[:, HALO + E_DEV:], 1, axis=0))
    grad_basis = jnp.sum(basis_parts, axis=0) * scale
    return (out_messages, result.reshape(N_EDGES * E_DEV, D), jnp.stack(layer_grads), grad_rev, grad_basis)
```

```python
import jax
import jax.numpy as jnp
from jax import lax
from jax.experimental import pallas as pl
from jax.experimental.pallas import tpu as pltpu
from jax.sharding import PartitionSpec as P

F32 = jnp.float32
BF16 = jnp.bfloat16
VMEM_LIMIT = 48 * 1024 * 1024


def split(value):
    high = value.astype(BF16)
    low = (value - high.astype(F32)).astype(BF16)
    return high, low


def dot(left, right, dims=((1,), (0,))):
    return lax.dot_general(left, right, (dims, ((), ())), preferred_element_type=F32)


def dot3(left, right, dims=((1,), (0,))):
    (lh, ll), (rh, rl) = left, right
    return dot(lh, rh, dims) + dot(lh, rl, dims) + dot(ll, rh, dims)


def pick(onehot, value):
    high, low = split(value)
    return dot(onehot, high) + dot(onehot, low)


def onehot_rows(column, width):
    ids = lax.broadcasted_iota(jnp.int32, (column.shape[0], width), 1)
    return jnp.where(column == ids, 1.0, 0.0).astype(BF16)


def onehot_columns(row, height):
    ids = lax.broadcasted_iota(jnp.int32, (height, row.shape[1]), 0)
    return jnp.where(row == ids, 1.0, 0.0).astype(BF16)


def silu_pair(values):
    sigma = jax.nn.sigmoid(values)
    return values * sigma, sigma * (1.0 + values * (1.0 - sigma))


def triplet_weight(basis, w_basis):
    bh, bl = split(basis)
    wh, wl = split(w_basis)
    return dot(
        jnp.concatenate([bh, bl, bh], axis=0),
        jnp.concatenate([wh, wh, wl], axis=0),
        ((0,), (0,)),
    )


def gather_window(low, messages, high, src_col):
    window = jnp.concatenate([low[...], messages[...], high[...]], axis=0)
    return pick(onehot_rows(src_col[...], window.shape[0]), window)


def agg_kernel(low, messages, high, src_col, tgt_row, basis, w_basis, agg):
    gathered = gather_window(low, messages, high, src_col)
    terms = gathered * triplet_weight(basis[...], w_basis[...])
    agg[...] = pick(onehot_columns(tgt_row[...], messages.shape[0]), terms)


def mlp_kernel(
    scale,
    messages,
    agg,
    r0,
    r1,
    r2,
    r3,
    slot_col,
    w_rev,
    w_layers,
    cotangent,
    out,
    grad0,
    grad_msg,
    grad_rev_proj,
    weight_grads,
):
    depth = w_layers.shape[0]
    group = r0.shape[0]
    highs, lows = [], []
    for k, arrived in enumerate((r0, r1, r2, r3)):
        onehot = onehot_rows(slot_col[k * group : (k + 1) * group, :], group)
        ah, al = split(arrived[...])
        highs.append(dot(onehot, ah).astype(BF16))
        lows.append(dot(onehot, al).astype(BF16))
    rev = (jnp.concatenate(highs, axis=0), jnp.concatenate(lows, axis=0))
    gate, rev_slope = silu_pair(dot3(rev, split(w_rev[...])))
    msg = messages[...]
    hidden = msg + agg[...] + msg * gate
    states, slopes, weights = [], [], []
    for layer in range(depth):
        state, weight = split(hidden), split(w_layers[layer])
        act, slope = silu_pair(dot3(state, weight))
        hidden = hidden + act
        states.append(state)
        slopes.append(slope)
        weights.append(weight)
    out[...] = hidden
    grad = cotangent[...]
    for layer in range(depth - 1, -1, -1):
        grad_pre = split(grad * slopes[layer])
        weight_grads[layer] = dot3(states[layer], grad_pre, ((0,), (0,))) * scale
        grad = grad + dot3(grad_pre, weights[layer], ((1,), (1,)))
    grad0[...] = grad
    grad_msg[...] = grad * (1.0 + gate)
    g_rev = grad * msg * rev_slope
    grad_rev_proj[...] = g_rev
    weight_grads[depth] = dot3(rev, split(g_rev), ((0,), (0,))) * scale


def back_kernel(
    scale,
    low,
    messages,
    high,
    src_col,
    src_row,
    tgt_col,
    basis,
    w_basis,
    grad0,
    window_grad,
    basis_grad,
):
    gathered = gather_window(low, messages, high, src_col)
    grad_prod = pick(onehot_rows(tgt_col[...], grad0.shape[0]), grad0[...])
    basis_grad[...] = dot3(split(basis[...]), split(grad_prod * gathered)) * scale
    terms = grad_prod * triplet_weight(basis[...], w_basis[...])
    window_grad[...] = pick(onehot_columns(src_row[...], window_grad.shape[0]), terms)


def end_kernel(
    grad_msg, window_grad, from_next, from_prev, b0, b1, b2, b3, slot_col, w_rev, out
):
    group = b0.shape[0]
    edges = out.shape[0]
    highs, lows = [], []
    for k, arrived in enumerate((b0, b1, b2, b3)):
        onehot = onehot_rows(slot_col[k * group : (k + 1) * group, :], group)
        ah, al = split(arrived[...])
        highs.append(dot(onehot, ah).astype(BF16))
        lows.append(dot(onehot, al).astype(BF16))
    returned = (jnp.concatenate(highs, axis=0), jnp.concatenate(lows, axis=0))
    out[...] = (
        grad_msg[...]
        + window_grad[group : group + edges, :]
        + dot3(returned, split(w_rev[...]), ((1,), (1,)))
    )
    out[:group, :] = out[:group, :] + from_prev[...]
    out[edges - group :, :] = out[edges - group :, :] + from_next[...]


def call(kernel, name, shapes, flops, *args):
    specs = [pl.BlockSpec(memory_space=pltpu.VMEM)]
    return pl.pallas_call(
        kernel,
        out_shape=[jax.ShapeDtypeStruct(shape, F32) for shape in shapes],
        in_specs=specs * len(args),
        out_specs=specs * len(shapes),
        cost_estimate=pl.CostEstimate(
            flops=flops, bytes_accessed=4 * 1024 * 1024, transcendentals=0
        ),
        compiler_params=pltpu.CompilerParams(vmem_limit_bytes=VMEM_LIMIT),
        name=name,
    )(*args)


def shift(block, distance):
    count = lax.axis_size("edges")
    return lax.ppermute(block, "edges", [(i, (i + distance) % count) for i in range(count)])


def exchange(rows):
    group = rows.shape[0] // 4
    count = lax.axis_size("edges")
    levels = count.bit_length() - 1
    arrived = []
    for k, bit in enumerate((0, levels // 3, 2 * levels // 3, levels - 1)):
        pairs = [(i, i ^ (1 << bit)) for i in range(count)]
        arrived.append(lax.ppermute(rows[k * group : (k + 1) * group], "edges", pairs))
    return arrived


def on_device(
    messages,
    rev_slot,
    tri_basis,
    tri_source,
    tri_target,
    tile_block,
    tile_count,
    w_basis,
    w_rev,
    w_layers,
    cotangent,
):
    edges, width = messages.shape
    halo = edges // 4
    depth = w_layers.shape[0]
    tiles = tile_block.shape[0]
    slots = tri_source.shape[0]
    scale = float(edges * lax.axis_size("edges")) ** (-0.5)
    low = shift(messages[edges - halo :], 1)
    high = shift(messages[:halo], -1)
    arrived = exchange(messages)

    live = jnp.arange(tiles, dtype=jnp.int32) < tile_count[0]
    target = tile_block[:, None] * 128 + tri_target.reshape(tiles, 128)
    target = jnp.where(live[:, None], target, -1)
    tgt_row, tgt_col = target.reshape(1, slots), target.reshape(slots, 1)
    src_row, src_col = tri_source.reshape(1, slots), tri_source.reshape(slots, 1)
    slot_col = rev_slot.reshape(edges, 1)

    (agg,) = call(
        agg_kernel,
        "agg",
        [(edges, width)],
        4 * slots * (2 * edges + 2 * halo) * width,
        low,
        messages,
        high,
        src_col,
        tgt_row,
        tri_basis,
        w_basis,
    )
    out, grad0, grad_msg, g_rev, weight_grads = call(
        lambda *refs: mlp_kernel(scale, *refs),
        "mlp",
        [(edges, width)] * 4 + [(depth + 1, width, width)],
        6 * 9 * edges * width * width,
        messages,
        agg,
        *arrived,
        slot_col,
        w_rev,
        w_layers,
        cotangent,
    )
    shares = lax.psum_scatter(weight_grads, "edges", scatter_dimension=1, tiled=True)
    shares = shares.reshape(depth + 1, -1)
    back = exchange(g_rev)
    window_grad, basis_grad = call(
        lambda *refs: back_kernel(scale, *refs),
        "back",
        [(edges + 2 * halo, width), w_basis.shape],
        4 * slots * (3 * edges + 4 * halo) * width,
        low,
        messages,
        high,
        src_col,
        src_row,
        tgt_col,
        tri_basis,
        w_basis,
        grad0,
    )
    from_next = shift(window_grad[:halo], -1)
    from_prev = shift(window_grad[halo + edges :], 1)
    grad_basis = lax.psum(basis_grad, "edges")
    (grad_out,) = call(
        end_kernel,
        "end",
        [(edges, width)],
        6 * edges * width * width,
        grad_msg,
        window_grad,
        from_next,
        from_prev,
        *back,
        slot_col,
        w_rev,
    )
    return (out, grad_out, shares[:depth], shares[depth], grad_basis)


def solution(mesh):
    in_specs = (
        P("edges", None),
        P("edges"),
        P(None, "edges"),
        P("edges"),
        P("edges"),
        P("edges"),
        P("edges"),
        P(),
        P(),
        P(),
        P("edges", None),
    )
    out_specs = (P("edges", None), P("edges", None), P(None, "edges"), P("edges"), P())
    return jax.shard_map(
        on_device, mesh=mesh, in_specs=in_specs, out_specs=out_specs, check_vma=False
    )
```

```python
import jax
import jax.numpy as jnp
from jax import lax
from jax.experimental import pallas as pl
from jax.experimental.pallas import tpu as pltpu
from jax.sharding import PartitionSpec as P

F32 = jnp.float32
BF16 = jnp.bfloat16
VMEM_LIMIT = 48 * 1024 * 1024


def split(value):
    high = value.astype(BF16)
    low = (value - high.astype(F32)).astype(BF16)
    return high, low


def dot(left, right, dims=((1,), (0,))):
    return lax.dot_general(left, right, (dims, ((), ())), preferred_element_type=F32)


def dot3(left, right, dims=((1,), (0,))):
    (lh, ll), (rh, rl) = left, right
    return dot(lh, rh, dims) + dot(lh, rl, dims) + dot(ll, rh, dims)


def pick(onehot, value):
    high, low = split(value)
    return dot(onehot, high) + dot(onehot, low)


def onehot_rows(column, width):
    ids = lax.broadcasted_iota(jnp.int32, (column.shape[0], width), 1)
    return jnp.where(column == ids, 1.0, 0.0).astype(BF16)


def onehot_columns(row, height):
    ids = lax.broadcasted_iota(jnp.int32, (height, row.shape[1]), 0)
    return jnp.where(row == ids, 1.0, 0.0).astype(BF16)


def silu_pair(values):
    sigma = jax.nn.sigmoid(values)
    return values * sigma, sigma * (1.0 + values * (1.0 - sigma))


def triplet_weight(basis, w_basis):
    bh, bl = split(basis)
    wh, wl = split(w_basis)
    return dot(
        jnp.concatenate([bh, bl, bh], axis=0),
        jnp.concatenate([wh, wh, wl], axis=0),
        ((0,), (0,)),
    )


def gather_window(low, messages, high, src_col):
    window = jnp.concatenate([low[...], messages[...], high[...]], axis=0)
    return pick(onehot_rows(src_col[...], window.shape[0]), window)


def agg_kernel(low, messages, high, src_col, tgt_row, basis, w_basis, agg):
    gathered = gather_window(low, messages, high, src_col)
    terms = gathered * triplet_weight(basis[...], w_basis[...])
    agg[...] = pick(onehot_columns(tgt_row[...], messages.shape[0]), terms)


def spread(target, index, value):
    devices, rows, half = target.shape[2:]
    for r, order in enumerate(routes(devices)):
        for shard in range(devices):
            target[index, r, place(shard, order)] = value[
                shard * rows : (shard + 1) * rows, r * half : (r + 1) * half
            ]


def mlp_kernel(
    scale,
    messages,
    agg,
    r0,
    r1,
    r2,
    r3,
    slot_col,
    w_rev,
    w_layers,
    cotangent,
    out,
    grad0,
    grad_msg,
    grad_rev_proj,
    weight_grads,
):
    depth = w_layers.shape[0]
    group = r0.shape[0]
    highs, lows = [], []
    for k, arrived in enumerate((r0, r1, r2, r3)):
        onehot = onehot_rows(slot_col[k * group : (k + 1) * group, :], group)
        ah, al = split(arrived[...])
        highs.append(dot(onehot, ah).astype(BF16))
        lows.append(dot(onehot, al).astype(BF16))
    rev = (jnp.concatenate(highs, axis=0), jnp.concatenate(lows, axis=0))
    gate, rev_slope = silu_pair(dot3(rev, split(w_rev[...])))
    msg = messages[...]
    hidden = msg + agg[...] + msg * gate
    states, slopes, weights = [], [], []
    for layer in range(depth):
        state, weight = split(hidden), split(w_layers[layer])
        act, slope = silu_pair(dot3(state, weight))
        hidden = hidden + act
        states.append(state)
        slopes.append(slope)
        weights.append(weight)
    out[...] = hidden
    grad = cotangent[...]
    for layer in range(depth - 1, -1, -1):
        grad_pre = split(grad * slopes[layer])
        spread(weight_grads, layer, dot3(states[layer], grad_pre, ((0,), (0,))) * scale)
        grad = grad + dot3(grad_pre, weights[layer], ((1,), (1,)))
    grad0[...] = grad
    grad_msg[...] = grad * (1.0 + gate)
    g_rev = grad * msg * rev_slope
    grad_rev_proj[...] = g_rev
    spread(weight_grads, depth, dot3(rev, split(g_rev), ((0,), (0,))) * scale)


def back_kernel(
    scale,
    low,
    messages,
    high,
    src_col,
    src_row,
    tgt_col,
    basis,
    w_basis,
    grad0,
    window_grad,
    basis_grad,
):
    gathered = gather_window(low, messages, high, src_col)
    grad_prod = pick(onehot_rows(tgt_col[...], grad0.shape[0]), grad0[...])
    basis_grad[...] = dot3(split(basis[...]), split(grad_prod * gathered)) * scale
    terms = grad_prod * triplet_weight(basis[...], w_basis[...])
    window_grad[...] = pick(onehot_columns(src_row[...], window_grad.shape[0]), terms)


def end_kernel(
    grad_msg, window_grad, from_next, from_prev, b0, b1, b2, b3, slot_col, w_rev, out
):
    group = b0.shape[0]
    edges = out.shape[0]
    highs, lows = [], []
    for k, arrived in enumerate((b0, b1, b2, b3)):
        onehot = onehot_rows(slot_col[k * group : (k + 1) * group, :], group)
        ah, al = split(arrived[...])
        highs.append(dot(onehot, ah).astype(BF16))
        lows.append(dot(onehot, al).astype(BF16))
    returned = (jnp.concatenate(highs, axis=0), jnp.concatenate(lows, axis=0))
    out[...] = (
        grad_msg[...]
        + window_grad[group : group + edges, :]
        + dot3(returned, split(w_rev[...]), ((1,), (1,)))
    )
    out[:group, :] = out[:group, :] + from_prev[...]
    out[edges - group :, :] = out[edges - group :, :] + from_next[...]


def routes(devices):
    levels = devices.bit_length() - 1
    first = list(range(levels))
    second = list(first)
    if levels > 2:
        second[1], second[2] = second[2], second[1]
    return first, second


def place(shard, order):
    spot = 0
    for bit in order:
        spot = 2 * spot + ((shard >> bit) & 1)
    return spot


def greet(me, levels):
    barrier = pltpu.get_barrier_semaphore()
    for bit in range(levels):
        pl.semaphore_signal(
            barrier, inc=1, device_id=(me ^ (1 << bit),), device_id_type=pl.DeviceIdType.MESH
        )
    pl.semaphore_wait(barrier, levels)


def send(source, target, send_sem, recv_sem, device):
    copy = pltpu.make_async_remote_copy(
        src_ref=source,
        dst_ref=target,
        send_sem=send_sem,
        recv_sem=recv_sem,
        device_id=(device,),
        device_id_type=pl.DeviceIdType.MESH,
    )
    copy.start()
    return copy


class Halving:
    def __init__(self, me, order, stages, inbox, send_sems, recv_sems):
        self.me, self.order = me, order
        self.stages, self.inbox = stages, inbox
        self.sems = (send_sems, recv_sems)
        self.copies = []

    def start(self, step):
        bit = self.order[step]
        count = self.stages[step].shape[0] // 2
        mine = (self.me // (1 << bit)) % 2
        self.mine, self.count = mine, count
        self.copies.append(
            send(
                self.stages[step].at[pl.ds((1 - mine) * count, count)],
                self.inbox[step],
                self.sems[0].at[step],
                self.sems[1].at[step],
                self.me ^ (1 << bit),
            )
        )

    def finish(self, step):
        self.copies[step].wait_recv()
        kept = self.stages[step][pl.ds(self.mine * self.count, self.count)]
        total = kept + self.inbox[step][...]
        if step + 1 < len(self.order):
            self.stages[step + 1][...] = total
        return total


def reduce_kernel(devices, parts, basis, layer_out, rev_out, basis_out, *scratch):
    levels = devices.bit_length() - 1
    matrices = parts.shape[0]
    rows, half = parts.shape[3], parts.shape[4]
    inboxes, scratch = scratch[:levels], scratch[levels:]
    kept, scratch = scratch[: levels - 1], scratch[levels - 1 :]
    basis_in, basis_sum, send_sems, recv_sems = scratch
    me = lax.axis_index("edges")
    greet(me, levels)
    orders = routes(devices)
    chains = []
    for m in range(matrices):
        for r in range(2):
            c = 2 * m + r
            stages = [parts.at[m, r]] + [ref.at[c] for ref in kept]
            inbox = [ref.at[c] for ref in inboxes]
            chains.append(
                Halving(me, orders[r], stages, inbox, send_sems.at[c], recv_sems.at[c])
            )
    last = len(chains)
    basis_sum[0] = basis[...]
    copies = []
    for step in range(levels):
        copies.append(
            send(
                basis_sum.at[step],
                basis_in.at[step],
                send_sems.at[last, step],
                recv_sems.at[last, step],
                me ^ (1 << step),
            )
        )
        for c, chain in enumerate(chains):
            if step:
                chain.finish(step - 1)
            chain.start(step)
        copies[step].wait_recv()
        basis_sum[step + 1] = basis_sum[step] + basis_in[step]
    for c, chain in enumerate(chains):
        total = chain.finish(levels - 1)
        m, r = c // 2, c % 2
        for row in range(rows):
            spot = slice(row * 2 * half + r * half, row * 2 * half + (r + 1) * half)
            if m + 1 < matrices:
                layer_out[m : m + 1, spot] = total[0, row : row + 1, :]
            else:
                rev_out[0:1, spot] = total[0, row : row + 1, :]
    basis_out[...] = basis_sum[levels]
    for chain in chains:
        for copy in chain.copies:
            copy.wait_send()
    for copy in copies:
        copy.wait_send()


def reduce_parts(parts, basis):
    devices = lax.axis_size("edges")
    levels = devices.bit_length() - 1
    matrices, lanes, _, rows, half = parts.shape
    chains = matrices * lanes
    flat = devices * rows * 2 * half // devices
    specs = [pl.BlockSpec(memory_space=pltpu.VMEM)]
    sizes = [devices >> (step + 1) for step in range(levels)]
    scratch = [pltpu.VMEM((chains, size, rows, half), F32) for size in sizes]
    scratch += [pltpu.VMEM((chains, size, rows, half), F32) for size in sizes[:-1]]
    scratch += [
        pltpu.VMEM((levels,) + basis.shape, F32),
        pltpu.VMEM((levels + 1,) + basis.shape, F32),
        pltpu.SemaphoreType.DMA((chains + 1, levels)),
        pltpu.SemaphoreType.DMA((chains + 1, levels)),
    ]
    return pl.pallas_call(
        lambda *refs: reduce_kernel(devices, *refs),
        out_shape=[
            jax.ShapeDtypeStruct((matrices - 1, flat), F32),
            jax.ShapeDtypeStruct((1, flat), F32),
            jax.ShapeDtypeStruct(basis.shape, F32),
        ],
        in_specs=specs * 2,
        out_specs=specs * 3,
        scratch_shapes=scratch,
        compiler_params=pltpu.CompilerParams(
            vmem_limit_bytes=VMEM_LIMIT, collective_id=0, has_side_effects=True
        ),
        name="reduce",
    )(parts, basis)


def call(kernel, name, shapes, flops, *args):
    specs = [pl.BlockSpec(memory_space=pltpu.VMEM)]
    return pl.pallas_call(
        kernel,
        out_shape=[jax.ShapeDtypeStruct(shape, F32) for shape in shapes],
        in_specs=specs * len(args),
        out_specs=specs * len(shapes),
        cost_estimate=pl.CostEstimate(
            flops=flops, bytes_accessed=4 * 1024 * 1024, transcendentals=0
        ),
        compiler_params=pltpu.CompilerParams(vmem_limit_bytes=VMEM_LIMIT),
        name=name,
    )(*args)


def shift(block, distance):
    count = lax.axis_size("edges")
    return lax.ppermute(block, "edges", [(i, (i + distance) % count) for i in range(count)])


def exchange(rows):
    group = rows.shape[0] // 4
    count = lax.axis_size("edges")
    levels = count.bit_length() - 1
    arrived = []
    for k, bit in enumerate((0, levels // 3, 2 * levels // 3, levels - 1)):
        pairs = [(i, i ^ (1 << bit)) for i in range(count)]
        arrived.append(lax.ppermute(rows[k * group : (k + 1) * group], "edges", pairs))
    return arrived


def on_device(
    messages,
    rev_slot,
    tri_basis,
    tri_source,
    tri_target,
    tile_block,
    tile_count,
    w_basis,
    w_rev,
    w_layers,
    cotangent,
):
    edges, width = messages.shape
    halo = edges // 4
    depth = w_layers.shape[0]
    tiles = tile_block.shape[0]
    slots = tri_source.shape[0]
    devices = lax.axis_size("edges")
    scale = float(edges * devices) ** (-0.5)
    low = shift(messages[edges - halo :], 1)
    high = shift(messages[:halo], -1)
    arrived = exchange(messages)

    live = jnp.arange(tiles, dtype=jnp.int32) < tile_count[0]
    target = tile_block[:, None] * 128 + tri_target.reshape(tiles, 128)
    target = jnp.where(live[:, None], target, -1)
    tgt_row, tgt_col = target.reshape(1, slots), target.reshape(slots, 1)
    src_row, src_col = tri_source.reshape(1, slots), tri_source.reshape(slots, 1)
    slot_col = rev_slot.reshape(edges, 1)

    (agg,) = call(
        agg_kernel,
        "agg",
        [(edges, width)],
        4 * slots * (2 * edges + 2 * halo) * width,
        low,
        messages,
        high,
        src_col,
        tgt_row,
        tri_basis,
        w_basis,
    )
    out, grad0, grad_msg, g_rev, weight_grads = call(
        lambda *refs: mlp_kernel(scale, *refs),
        "mlp",
        [(edges, width)] * 4
        + [(depth + 1, 2, devices, width // devices, width // 2)],
        6 * 9 * edges * width * width,
        messages,
        agg,
        *arrived,
        slot_col,
        w_rev,
        w_layers,
        cotangent,
    )
    back = exchange(g_rev)
    window_grad, basis_grad = call(
        lambda *refs: back_kernel(scale, *refs),
        "back",
        [(edges + 2 * halo, width), w_basis.shape],
        4 * slots * (3 * edges + 4 * halo) * width,
        low,
        messages,
        high,
        src_col,
        src_row,
        tgt_col,
        tri_basis,
        w_basis,
        grad0,
    )
    from_next = shift(window_grad[:halo], -1)
    from_prev = shift(window_grad[halo + edges :], 1)
    layer_share, rev_share, grad_basis = reduce_parts(weight_grads, basis_grad)
    (grad_out,) = call(
        end_kernel,
        "end",
        [(edges, width)],
        6 * edges * width * width,
        grad_msg,
        window_grad,
        from_next,
        from_prev,
        *back,
        slot_col,
        w_rev,
    )
    return (out, grad_out, layer_share, rev_share.reshape(-1), grad_basis)


def solution(mesh):
    in_specs = (
        P("edges", None),
        P("edges"),
        P(None, "edges"),
        P("edges"),
        P("edges"),
        P("edges"),
        P("edges"),
        P(),
        P(),
        P(),
        P("edges", None),
    )
    out_specs = (P("edges", None), P("edges", None), P(None, "edges"), P("edges"), P())
    return jax.shard_map(
        on_device, mesh=mesh, in_specs=in_specs, out_specs=out_specs, check_vma=False
    )
```

```python
import jax
import jax.numpy as jnp
from jax import lax
from jax.experimental import pallas as pl
from jax.experimental.pallas import tpu as pltpu
from jax.sharding import PartitionSpec as P

F32 = jnp.float32
BF16 = jnp.bfloat16
VMEM_LIMIT = 56 * 1024 * 1024


def split(value):
    high = value.astype(BF16)
    low = (value - high.astype(F32)).astype(BF16)
    return high, low


def dot(left, right, dims=((1,), (0,))):
    return lax.dot_general(left, right, (dims, ((), ())), preferred_element_type=F32)


def dot3(left, right, dims=((1,), (0,))):
    (lh, ll), (rh, rl) = left, right
    return dot(lh, rh, dims) + dot(lh, rl, dims) + dot(ll, rh, dims)


def pick(onehot, value):
    high, low = split(value)
    return dot(onehot, high) + dot(onehot, low)


def onehot_rows(column, width):
    ids = lax.broadcasted_iota(jnp.int32, (column.shape[0], width), 1)
    return jnp.where(column == ids, 1.0, 0.0).astype(BF16)


def onehot_columns(row, height):
    ids = lax.broadcasted_iota(jnp.int32, (height, row.shape[1]), 0)
    return jnp.where(row == ids, 1.0, 0.0).astype(BF16)


def silu_pair(values):
    sigma = jax.nn.sigmoid(values)
    return values * sigma, sigma * (1.0 + values * (1.0 - sigma))


def triplet_weight(basis, w_basis):
    bh, bl = split(basis)
    wh, wl = split(w_basis)
    return dot(
        jnp.concatenate([bh, bl, bh], axis=0),
        jnp.concatenate([wh, wh, wl], axis=0),
        ((0,), (0,)),
    )


def spread(target, index, value):
    devices, rows, half = target.shape[2:]
    for r, order in enumerate(routes(devices)):
        for shard in range(devices):
            target[index, r, place(shard, order)] = value[
                shard * rows : (shard + 1) * rows, r * half : (r + 1) * half
            ]


def routes(devices):
    levels = devices.bit_length() - 1
    first = list(range(levels))
    second = list(first)
    if levels > 2:
        second[1], second[2] = second[2], second[1]
    return first, second


def place(shard, order):
    spot = 0
    for bit in order:
        spot = 2 * spot + ((shard >> bit) & 1)
    return spot


def send(source, target, send_sem, recv_sem, device):
    copy = pltpu.make_async_remote_copy(
        src_ref=source,
        dst_ref=target,
        send_sem=send_sem,
        recv_sem=recv_sem,
        device_id=(device,),
        device_id_type=pl.DeviceIdType.MESH,
    )
    copy.start()
    return copy


def greet(me, devices):
    levels = devices.bit_length() - 1
    barrier = pltpu.get_barrier_semaphore()
    others = [me ^ (1 << bit) for bit in range(levels)]
    others += [lax.rem(me + 1, devices), lax.rem(me + devices - 1, devices)]
    for other in others:
        pl.semaphore_signal(
            barrier, inc=1, device_id=(other,), device_id_type=pl.DeviceIdType.MESH
        )
    pl.semaphore_wait(barrier, len(others))


class Halving:
    def __init__(self, me, order, stages, inbox, send_sems, recv_sems):
        self.me, self.order = me, order
        self.stages, self.inbox = stages, inbox
        self.sems = (send_sems, recv_sems)
        self.copies = []

    def start(self, step):
        bit = self.order[step]
        count = self.stages[step].shape[0] // 2
        mine = (self.me // (1 << bit)) % 2
        self.mine, self.count = mine, count
        self.copies.append(
            send(
                self.stages[step].at[pl.ds((1 - mine) * count, count)],
                self.inbox[step],
                self.sems[0].at[step],
                self.sems[1].at[step],
                self.me ^ (1 << bit),
            )
        )

    def finish(self, step):
        self.copies[step].wait_recv()
        kept = self.stages[step][pl.ds(self.mine * self.count, self.count)]
        total = kept + self.inbox[step][...]
        if step + 1 < len(self.order):
            self.stages[step + 1][...] = total
        return total

    def advance(self):
        step = len(self.copies)
        if step < len(self.order):
            if step:
                self.finish(step - 1)
            self.start(step)


def block_kernel(
    devices,
    scale,
    messages,
    src_col,
    src_row,
    tgt_col,
    tgt_row,
    slot_col,
    basis,
    w_basis,
    w_rev,
    w_layers,
    cotangent,
    out,
    grad_out,
    layer_out,
    rev_out,
    basis_out,
    *scratch,
):
    levels = devices.bit_length() - 1
    edges, width = messages.shape
    halo = group = edges // 4
    depth = w_layers.shape[0]
    inboxes, scratch = scratch[:levels], scratch[levels:]
    kept, scratch = scratch[: levels - 1], scratch[levels - 1 :]
    (
        parts,
        window,
        arrived,
        returned,
        g_rev,
        gathered,
        tri_weight,
        window_grad,
        rims,
        basis_in,
        basis_sum,
        send_sems,
        recv_sems,
        row_send,
        row_recv,
    ) = scratch
    me = lax.axis_index("edges")
    ahead, behind = lax.rem(me + 1, devices), lax.rem(me + devices - 1, devices)
    bits = (0, levels // 3, 2 * levels // 3, levels - 1)
    greet(me, devices)

    def row_copy(source, target, slot, device):
        return send(source, target, row_send.at[slot], row_recv.at[slot], device)

    halos = [
        row_copy(messages.at[pl.ds(edges - halo, halo)], window.at[pl.ds(0, halo)], 0, ahead),
        row_copy(
            messages.at[pl.ds(0, halo)], window.at[pl.ds(halo + edges, halo)], 1, behind
        ),
    ]

    def exchange(rows, target, first):
        copies = [None] * 4
        for k in (3, 2, 1, 0):
            copies[k] = row_copy(
                rows.at[pl.ds(k * group, group)], target.at[k], first + k, me ^ (1 << bits[k])
            )
        return copies

    def collect(copies, target):
        highs, lows = [], []
        for k in range(4):
            onehot = onehot_rows(slot_col[k * group : (k + 1) * group, :], group)
            copies[k].wait_recv()
            ah, al = split(target[k])
            highs.append(dot(onehot, ah).astype(BF16))
            lows.append(dot(onehot, al).astype(BF16))
        return jnp.concatenate(highs, axis=0), jnp.concatenate(lows, axis=0)

    forth = exchange(messages, arrived, 2)
    window[halo : halo + edges, :] = messages[...]
    tri_weight[...] = triplet_weight(basis[...], w_basis[...])
    weights = [split(w_layers[layer]) for layer in range(depth)]
    weight_rev = split(w_rev[...])
    for copy in halos:
        copy.wait_recv()
    gathered[...] = pick(onehot_rows(src_col[...], edges + 2 * halo), window[...])
    agg = pick(onehot_columns(tgt_row[...], edges), gathered[...] * tri_weight[...])

    rev = collect(forth, arrived)
    gate, rev_slope = silu_pair(dot3(rev, weight_rev))
    msg = messages[...]
    hidden = msg + agg + msg * gate
    states, slopes, grad_pres = [], [], [None] * depth
    for layer in range(depth):
        state = split(hidden)
        act, slope = silu_pair(dot3(state, weights[layer]))
        hidden = hidden + act
        states.append(state)
        slopes.append(slope)
    out[...] = hidden
    grad = cotangent[...]
    for layer in range(depth - 1, -1, -1):
        grad_pres[layer] = split(grad * slopes[layer])
        grad = grad + dot3(grad_pres[layer], weights[layer], ((1,), (1,)))
    g_rev_rows = grad * msg * rev_slope
    g_rev[...] = g_rev_rows
    back = exchange(g_rev, returned, 6)
    grad_out[...] = grad * (1.0 + gate)

    orders = routes(devices)
    chains = []
    for m in range(depth + 1):
        for r in range(2):
            c = 2 * m + r
            stages = [parts.at[m, r]] + [ref.at[c] for ref in kept]
            inbox = [ref.at[c] for ref in inboxes]
            chains.append(
                Halving(me, orders[r], stages, inbox, send_sems.at[c], recv_sems.at[c])
            )

    def advance(m):
        chains[2 * m].advance()
        chains[2 * m + 1].advance()

    for layer in range(depth - 1, -1, -1):
        product = dot3(states[layer], grad_pres[layer], ((0,), (0,)))
        spread(parts, layer, product * scale)
        for m in range(depth - 1, layer - 1, -1):
            advance(m)
    spread(parts, depth, dot3(rev, split(g_rev_rows), ((0,), (0,))) * scale)
    advance(depth)
    advance(0)
    grad_prod = pick(onehot_rows(tgt_col[...], edges), grad)
    basis_sum[0] = dot3(split(basis[...]), split(grad_prod * gathered[...])) * scale
    last = len(chains)
    basis_copies = []

    def basis_advance():
        step = len(basis_copies)
        if step:
            basis_copies[-1].wait_recv()
            basis_sum[step] = basis_sum[step - 1] + basis_in[step - 1]
        if step < levels:
            basis_copies.append(
                send(
                    basis_sum.at[step],
                    basis_in.at[step],
                    send_sems.at[last, step],
                    recv_sems.at[last, step],
                    me ^ (1 << step),
                )
            )

    basis_advance()
    advance(depth)
    window_grad[...] = pick(
        onehot_columns(src_row[...], edges + 2 * halo), grad_prod * tri_weight[...]
    )
    rim_copies = [
        row_copy(window_grad.at[pl.ds(0, halo)], rims.at[0], 10, behind),
        row_copy(window_grad.at[pl.ds(halo + edges, halo)], rims.at[1], 11, ahead),
    ]
    for m in range(depth - 1, -1, -1):
        advance(m)
    basis_advance()
    grad_out[...] = (
        grad_out[...]
        + window_grad[halo : halo + edges, :]
        + dot3(collect(back, returned), weight_rev, ((1,), (1,)))
    )
    advance(depth)
    for step in range(2, levels):
        for m in list(range(depth - 1, -1, -1)) + [depth]:
            advance(m)
        basis_advance()
    rim_copies[0].wait_recv()
    grad_out[edges - halo :, :] = grad_out[edges - halo :, :] + rims[0]
    rim_copies[1].wait_recv()
    grad_out[:halo, :] = grad_out[:halo, :] + rims[1]
    rows, half = parts.shape[3], parts.shape[4]
    for c, chain in enumerate(chains):
        while len(chain.copies) < levels:
            chain.advance()
        total = chain.finish(levels - 1)
        m, r = c // 2, c % 2
        for row in range(rows):
            spot = slice(row * width + r * half, row * width + (r + 1) * half)
            if m < depth:
                layer_out[m : m + 1, spot] = total[0, row : row + 1, :]
            else:
                rev_out[0:1, spot] = total[0, row : row + 1, :]
    basis_advance()
    basis_out[...] = basis_sum[levels]
    for copy in halos + forth + back + rim_copies + basis_copies:
        copy.wait_send()
    for chain in chains:
        for copy in chain.copies:
            copy.wait_send()


def on_device(
    messages,
    rev_slot,
    tri_basis,
    tri_source,
    tri_target,
    tile_block,
    tile_count,
    w_basis,
    w_rev,
    w_layers,
    cotangent,
):
    devices = lax.axis_size("edges")
    levels = devices.bit_length() - 1
    edges, width = messages.shape
    halo = edges // 4
    depth = w_layers.shape[0]
    tiles = tile_block.shape[0]
    slots = tri_source.shape[0]
    scale = float(edges * devices) ** (-0.5)

    live = jnp.arange(tiles, dtype=jnp.int32) < tile_count[0]
    target = tile_block[:, None] * 128 + tri_target.reshape(tiles, 128)
    target = jnp.where(live[:, None], target, -1)
    tgt_row, tgt_col = target.reshape(1, slots), target.reshape(slots, 1)
    src_row, src_col = tri_source.reshape(1, slots), tri_source.reshape(slots, 1)
    slot_col = rev_slot.reshape(edges, 1)

    rows, half, chains = width // devices, width // 2, 2 * (depth + 1)
    sizes = [devices >> (step + 1) for step in range(levels)]
    scratch = [pltpu.VMEM((chains, size, rows, half), F32) for size in sizes]
    scratch += [pltpu.VMEM((chains, size, rows, half), F32) for size in sizes[:-1]]
    scratch += [
        pltpu.VMEM((depth + 1, 2, devices, rows, half), F32),
        pltpu.VMEM((edges + 2 * halo, width), F32),
        pltpu.VMEM((4, halo, width), F32),
        pltpu.VMEM((4, halo, width), F32),
        pltpu.VMEM((edges, width), F32),
        pltpu.VMEM((slots, width), F32),
        pltpu.VMEM((slots, width), F32),
        pltpu.VMEM((edges + 2 * halo, width), F32),
        pltpu.VMEM((2, halo, width), F32),
        pltpu.VMEM((levels,) + w_basis.shape, F32),
        pltpu.VMEM((levels + 1,) + w_basis.shape, F32),
        pltpu.SemaphoreType.DMA((chains + 1, levels)),
        pltpu.SemaphoreType.DMA((chains + 1, levels)),
        pltpu.SemaphoreType.DMA((12,)),
        pltpu.SemaphoreType.DMA((12,)),
    ]
    shapes = [
        (edges, width),
        (edges, width),
        (depth, width * rows),
        (1, width * rows),
        w_basis.shape,
    ]
    specs = [pl.BlockSpec(memory_space=pltpu.VMEM)]
    out, grad_out, layer_share, rev_share, grad_basis = pl.pallas_call(
        lambda *refs: block_kernel(devices, scale, *refs),
        out_shape=[jax.ShapeDtypeStruct(shape, F32) for shape in shapes],
        in_specs=specs * 11,
        out_specs=specs * 5,
        scratch_shapes=scratch,
        compiler_params=pltpu.CompilerParams(
            vmem_limit_bytes=VMEM_LIMIT, collective_id=0, has_side_effects=True
        ),
        name="block",
    )(
        messages,
        src_col,
        src_row,
        tgt_col,
        tgt_row,
        slot_col,
        tri_basis,
        w_basis,
        w_rev,
        w_layers,
        cotangent,
    )
    return (out, grad_out, layer_share, rev_share.reshape(-1), grad_basis)


def solution(mesh):
    in_specs = (
        P("edges", None),
        P("edges"),
        P(None, "edges"),
        P("edges"),
        P("edges"),
        P("edges"),
        P("edges"),
        P(),
        P(),
        P(),
        P("edges", None),
    )
    out_specs = (P("edges", None), P("edges", None), P(None, "edges"), P("edges"), P())
    return jax.shard_map(
        on_device, mesh=mesh, in_specs=in_specs, out_specs=out_specs, check_vma=False
    )
```

```python
import jax
import jax.numpy as jnp
from jax import lax
from jax.experimental import pallas as pl
from jax.experimental.pallas import tpu as pltpu
from jax.sharding import PartitionSpec as P

F32 = jnp.float32
BF16 = jnp.bfloat16
VMEM_LIMIT = 56 * 1024 * 1024


def split(value):
    high = value.astype(BF16)
    low = (value - high.astype(F32)).astype(BF16)
    return high, low


def dot(left, right, dims=((1,), (0,))):
    return lax.dot_general(left, right, (dims, ((), ())), preferred_element_type=F32)


def dot3(left, right, dims=((1,), (0,))):
    (lh, ll), (rh, rl) = left, right
    return dot(lh, rh, dims) + dot(lh, rl, dims) + dot(ll, rh, dims)


def pick(onehot, value):
    high, low = split(value)
    return dot(onehot, high) + dot(onehot, low)


def onehot_rows(column, width):
    ids = lax.broadcasted_iota(jnp.int32, (column.shape[0], width), 1)
    return jnp.where(column == ids, 1.0, 0.0).astype(BF16)


def column_of(row):
    return jnp.broadcast_to(row, (8, row.shape[1])).T[:, :1]


def onehot_columns(row, height):
    ids = lax.broadcasted_iota(jnp.int32, (height, row.shape[1]), 0)
    return jnp.where(row == ids, 1.0, 0.0).astype(BF16)


def silu_pair(values):
    sigma = jax.nn.sigmoid(values)
    return values * sigma, sigma * (1.0 + values * (1.0 - sigma))


def triplet_weight(basis, w_basis):
    bh, bl = split(basis)
    wh, wl = split(w_basis)
    return dot(
        jnp.concatenate([bh, bl, bh], axis=0),
        jnp.concatenate([wh, wh, wl], axis=0),
        ((0,), (0,)),
    )


def spread(target, index, value):
    devices, rows, half = target.shape[2:]
    for r, order in enumerate(routes(devices)):
        for shard in range(devices):
            target[index, r, place(shard, order)] = value[
                shard * rows : (shard + 1) * rows, r * half : (r + 1) * half
            ]


def routes(devices):
    levels = devices.bit_length() - 1
    first = list(range(levels))
    second = list(first)
    if levels > 2:
        second[1], second[2] = second[2], second[1]
    return first, second


def place(shard, order):
    spot = 0
    for bit in order:
        spot = 2 * spot + ((shard >> bit) & 1)
    return spot


def send(source, target, send_sem, recv_sem, device):
    copy = pltpu.make_async_remote_copy(
        src_ref=source,
        dst_ref=target,
        send_sem=send_sem,
        recv_sem=recv_sem,
        device_id=(device,),
        device_id_type=pl.DeviceIdType.MESH,
    )
    copy.start()
    return copy


def greet(me, devices):
    levels = devices.bit_length() - 1
    barrier = pltpu.get_barrier_semaphore()
    others = [me ^ (1 << bit) for bit in range(levels)]
    others += [lax.rem(me + 1, devices), lax.rem(me + devices - 1, devices)]
    for other in others:
        pl.semaphore_signal(
            barrier, inc=1, device_id=(other,), device_id_type=pl.DeviceIdType.MESH
        )
    pl.semaphore_wait(barrier, len(others))


class Halving:
    def __init__(self, me, order, stages, inbox, send_sems, recv_sems):
        self.me, self.order = me, order
        self.stages, self.inbox = stages, inbox
        self.sems = (send_sems, recv_sems)
        self.copies = []

    def start(self, step):
        bit = self.order[step]
        count = self.stages[step].shape[0] // 2
        mine = (self.me // (1 << bit)) % 2
        self.mine, self.count = mine, count
        self.copies.append(
            send(
                self.stages[step].at[pl.ds((1 - mine) * count, count)],
                self.inbox[step],
                self.sems[0].at[step],
                self.sems[1].at[step],
                self.me ^ (1 << bit),
            )
        )

    def finish(self, step):
        self.copies[step].wait_recv()
        kept = self.stages[step][pl.ds(self.mine * self.count, self.count)]
        total = kept + self.inbox[step][...]
        if step + 1 < len(self.order):
            self.stages[step + 1][...] = total
        return total

    def advance(self):
        step = len(self.copies)
        if step < len(self.order):
            if step:
                self.finish(step - 1)
            self.start(step)


def block_kernel(
    devices,
    scale,
    messages,
    src_row,
    tgt_row,
    slot_row,
    basis,
    w_basis,
    w_rev,
    w_layers,
    cotangent,
    out,
    grad_out,
    layer_out,
    rev_out,
    basis_out,
    *scratch,
):
    levels = devices.bit_length() - 1
    edges, width = messages.shape
    halo = group = edges // 4
    depth = w_layers.shape[0]
    inboxes, scratch = scratch[:levels], scratch[levels:]
    kept, scratch = scratch[: levels - 1], scratch[levels - 1 :]
    (
        parts,
        window,
        arrived,
        returned,
        g_rev,
        gathered,
        tri_weight,
        window_grad,
        rims,
        basis_in,
        basis_sum,
        send_sems,
        recv_sems,
        row_send,
        row_recv,
    ) = scratch
    me = lax.axis_index("edges")
    ahead, behind = lax.rem(me + 1, devices), lax.rem(me + devices - 1, devices)
    bits = (0, levels // 3, 2 * levels // 3, levels - 1)
    greet(me, devices)

    def row_copy(source, target, slot, device):
        return send(source, target, row_send.at[slot], row_recv.at[slot], device)

    halos = [
        row_copy(messages.at[pl.ds(edges - halo, halo)], window.at[pl.ds(0, halo)], 0, ahead),
        row_copy(
            messages.at[pl.ds(0, halo)], window.at[pl.ds(halo + edges, halo)], 1, behind
        ),
    ]

    def exchange(rows, target, first):
        copies = [None] * 4
        for k in (3, 2, 1, 0):
            copies[k] = row_copy(
                rows.at[pl.ds(k * group, group)], target.at[k], first + k, me ^ (1 << bits[k])
            )
        return copies

    def collect(copies, target):
        highs, lows = [], []
        for k in range(4):
            onehot = onehot_rows(slot_col[k * group : (k + 1) * group, :], group)
            copies[k].wait_recv()
            ah, al = split(target[k])
            highs.append(dot(onehot, ah).astype(BF16))
            lows.append(dot(onehot, al).astype(BF16))
        return jnp.concatenate(highs, axis=0), jnp.concatenate(lows, axis=0)

    forth = exchange(messages, arrived, 2)
    src_col, tgt_col = column_of(src_row[...]), column_of(tgt_row[...])
    slot_col = column_of(slot_row[...])
    window[halo : halo + edges, :] = messages[...]
    tri_weight[...] = triplet_weight(basis[...], w_basis[...])
    weights = [split(w_layers[layer]) for layer in range(depth)]
    weight_rev = split(w_rev[...])
    for copy in halos:
        copy.wait_recv()
    gathered[...] = pick(onehot_rows(src_col, edges + 2 * halo), window[...])
    agg = pick(onehot_columns(tgt_row[...], edges), gathered[...] * tri_weight[...])

    rev = collect(forth, arrived)
    gate, rev_slope = silu_pair(dot3(rev, weight_rev))
    msg = messages[...]
    hidden = msg + agg + msg * gate
    states, slopes, grad_pres = [], [], [None] * depth
    for layer in range(depth):
        state = split(hidden)
        act, slope = silu_pair(dot3(state, weights[layer]))
        hidden = hidden + act
        states.append(state)
        slopes.append(slope)
    out[...] = hidden
    grad = cotangent[...]
    for layer in range(depth - 1, -1, -1):
        grad_pres[layer] = split(grad * slopes[layer])
        grad = grad + dot3(grad_pres[layer], weights[layer], ((1,), (1,)))
    g_rev_rows = grad * msg * rev_slope
    g_rev[...] = g_rev_rows
    back = exchange(g_rev, returned, 6)
    grad_out[...] = grad * (1.0 + gate)

    orders = routes(devices)
    chains = []
    for m in range(depth + 1):
        for r in range(2):
            c = 2 * m + r
            stages = [parts.at[m, r]] + [ref.at[c] for ref in kept]
            inbox = [ref.at[c] for ref in inboxes]
            chains.append(
                Halving(me, orders[r], stages, inbox, send_sems.at[c], recv_sems.at[c])
            )

    def advance(m):
        chains[2 * m].advance()
        chains[2 * m + 1].advance()

    for layer in range(depth - 1, -1, -1):
        product = dot3(states[layer], grad_pres[layer], ((0,), (0,)))
        spread(parts, layer, product * scale)
        for m in range(depth - 1, layer - 1, -1):
            advance(m)
    spread(parts, depth, dot3(rev, split(g_rev_rows), ((0,), (0,))) * scale)
    advance(depth)
    advance(0)
    grad_prod = pick(onehot_rows(tgt_col, edges), grad)
    basis_sum[0] = dot3(split(basis[...]), split(grad_prod * gathered[...])) * scale
    last = len(chains)
    basis_copies = []

    def basis_advance():
        step = len(basis_copies)
        if step:
            basis_copies[-1].wait_recv()
            basis_sum[step] = basis_sum[step - 1] + basis_in[step - 1]
        if step < levels:
            basis_copies.append(
                send(
                    basis_sum.at[step],
                    basis_in.at[step],
                    send_sems.at[last, step],
                    recv_sems.at[last, step],
                    me ^ (1 << step),
                )
            )

    basis_advance()
    advance(depth)
    window_grad[...] = pick(
        onehot_columns(src_row[...], edges + 2 * halo), grad_prod * tri_weight[...]
    )
    rim_copies = [
        row_copy(window_grad.at[pl.ds(0, halo)], rims.at[0], 10, behind),
        row_copy(window_grad.at[pl.ds(halo + edges, halo)], rims.at[1], 11, ahead),
    ]
    for m in range(depth - 1, -1, -1):
        advance(m)
    basis_advance()
    grad_out[...] = (
        grad_out[...]
        + window_grad[halo : halo + edges, :]
        + dot3(collect(back, returned), weight_rev, ((1,), (1,)))
    )
    advance(depth)
    for step in range(2, levels):
        for m in list(range(depth - 1, -1, -1)) + [depth]:
            advance(m)
        basis_advance()
    rim_copies[0].wait_recv()
    grad_out[edges - halo :, :] = grad_out[edges - halo :, :] + rims[0]
    rim_copies[1].wait_recv()
    grad_out[:halo, :] = grad_out[:halo, :] + rims[1]
    rows, half = parts.shape[3], parts.shape[4]
    for c, chain in enumerate(chains):
        while len(chain.copies) < levels:
            chain.advance()
        total = chain.finish(levels - 1)
        m, r = c // 2, c % 2
        for row in range(rows):
            spot = slice(row * width + r * half, row * width + (r + 1) * half)
            if m < depth:
                layer_out[m : m + 1, spot] = total[0, row : row + 1, :]
            else:
                rev_out[0:1, spot] = total[0, row : row + 1, :]
    basis_advance()
    basis_out[...] = basis_sum[levels]
    for copy in halos + forth + back + rim_copies + basis_copies:
        copy.wait_send()
    for chain in chains:
        for copy in chain.copies:
            copy.wait_send()


def on_device(
    messages,
    rev_slot,
    tri_basis,
    tri_source,
    tri_target,
    tile_block,
    tile_count,
    w_basis,
    w_rev,
    w_layers,
    cotangent,
):
    devices = lax.axis_size("edges")
    levels = devices.bit_length() - 1
    edges, width = messages.shape
    halo = edges // 4
    depth = w_layers.shape[0]
    tiles = tile_block.shape[0]
    slots = tri_source.shape[0]
    scale = float(edges * devices) ** (-0.5)

    live = jnp.arange(tiles, dtype=jnp.int32) < tile_count[0]
    target = tile_block[:, None] * 128 + tri_target.reshape(tiles, 128)
    target = jnp.where(live[:, None], target, -1)
    tgt_row = target.reshape(1, slots)
    src_row = tri_source.reshape(1, slots)
    slot_row = rev_slot.reshape(1, edges)

    rows, half, chains = width // devices, width // 2, 2 * (depth + 1)
    sizes = [devices >> (step + 1) for step in range(levels)]
    scratch = [pltpu.VMEM((chains, size, rows, half), F32) for size in sizes]
    scratch += [pltpu.VMEM((chains, size, rows, half), F32) for size in sizes[:-1]]
    scratch += [
        pltpu.VMEM((depth + 1, 2, devices, rows, half), F32),
        pltpu.VMEM((edges + 2 * halo, width), F32),
        pltpu.VMEM((4, halo, width), F32),
        pltpu.VMEM((4, halo, width), F32),
        pltpu.VMEM((edges, width), F32),
        pltpu.VMEM((slots, width), F32),
        pltpu.VMEM((slots, width), F32),
        pltpu.VMEM((edges + 2 * halo, width), F32),
        pltpu.VMEM((2, halo, width), F32),
        pltpu.VMEM((levels,) + w_basis.shape, F32),
        pltpu.VMEM((levels + 1,) + w_basis.shape, F32),
        pltpu.SemaphoreType.DMA((chains + 1, levels)),
        pltpu.SemaphoreType.DMA((chains + 1, levels)),
        pltpu.SemaphoreType.DMA((12,)),
        pltpu.SemaphoreType.DMA((12,)),
    ]
    shapes = [
        (edges, width),
        (edges, width),
        (depth, width * rows),
        (1, width * rows),
        w_basis.shape,
    ]
    specs = [pl.BlockSpec(memory_space=pltpu.VMEM)]
    out, grad_out, layer_share, rev_share, grad_basis = pl.pallas_call(
        lambda *refs: block_kernel(devices, scale, *refs),
        out_shape=[jax.ShapeDtypeStruct(shape, F32) for shape in shapes],
        in_specs=specs * 9,
        out_specs=specs * 5,
        scratch_shapes=scratch,
        compiler_params=pltpu.CompilerParams(
            vmem_limit_bytes=VMEM_LIMIT, collective_id=0, has_side_effects=True
        ),
        name="block",
    )(
        messages,
        src_row,
        tgt_row,
        slot_row,
        tri_basis,
        w_basis,
        w_rev,
        w_layers,
        cotangent,
    )
    return (out, grad_out, layer_share, rev_share.reshape(-1), grad_basis)


def solution(mesh):
    in_specs = (
        P("edges", None),
        P("edges"),
        P(None, "edges"),
        P("edges"),
        P("edges"),
        P("edges"),
        P("edges"),
        P(),
        P(),
        P(),
        P("edges", None),
    )
    out_specs = (P("edges", None), P("edges", None), P(None, "edges"), P("edges"), P())
    return jax.shard_map(
        on_device, mesh=mesh, in_specs=in_specs, out_specs=out_specs, check_vma=False
    )
```

```python
import jax
import jax.numpy as jnp
from jax import lax
from jax.experimental import pallas as pl
from jax.experimental.pallas import tpu as pltpu
from jax.sharding import PartitionSpec as P

F32 = jnp.float32
BF16 = jnp.bfloat16
VMEM_LIMIT = 56 * 1024 * 1024


def split(value):
    high = value.astype(BF16)
    low = (value - high.astype(F32)).astype(BF16)
    return high, low


def dot(left, right, dims=((1,), (0,))):
    return lax.dot_general(left, right, (dims, ((), ())), preferred_element_type=F32)


def dot3(left, right, dims=((1,), (0,))):
    (lh, ll), (rh, rl) = left, right
    return dot(lh, rh, dims) + dot(lh, rl, dims) + dot(ll, rh, dims)


def pick(onehot, value):
    high, low = split(value)
    return dot(onehot, high) + dot(onehot, low)


def onehot_rows(column, width):
    ids = lax.broadcasted_iota(jnp.int32, (column.shape[0], width), 1)
    return jnp.where(column == ids, 1.0, 0.0).astype(BF16)


def column_of(row):
    return jnp.broadcast_to(row, (8, row.shape[1])).T[:, :1]


def onehot_columns(row, height):
    ids = lax.broadcasted_iota(jnp.int32, (height, row.shape[1]), 0)
    return jnp.where(row == ids, 1.0, 0.0).astype(BF16)


def silu_pair(values):
    sigma = jax.nn.sigmoid(values)
    return values * sigma, sigma * (1.0 + values * (1.0 - sigma))


def triplet_weight(basis, w_basis):
    bh, bl = split(basis)
    wh, wl = split(w_basis)
    return dot(
        jnp.concatenate([bh, bl, bh], axis=0),
        jnp.concatenate([wh, wh, wl], axis=0),
        ((0,), (0,)),
    )


def spread(target, index, value):
    devices, rows, half = target.shape[2:]
    for r, order in enumerate(routes(devices)):
        for shard in range(devices):
            target[index, r, place(shard, order)] = value[
                shard * rows : (shard + 1) * rows, r * half : (r + 1) * half
            ]


def routes(devices):
    levels = devices.bit_length() - 1
    first = list(range(levels))
    second = list(first)
    if levels > 2:
        second[1], second[2] = second[2], second[1]
    return first, second


def place(shard, order):
    spot = 0
    for bit in order:
        spot = 2 * spot + ((shard >> bit) & 1)
    return spot


def send(source, target, send_sem, recv_sem, device):
    copy = pltpu.make_async_remote_copy(
        src_ref=source,
        dst_ref=target,
        send_sem=send_sem,
        recv_sem=recv_sem,
        device_id=(device,),
        device_id_type=pl.DeviceIdType.MESH,
    )
    copy.start()
    return copy


def greet(me, devices):
    levels = devices.bit_length() - 1
    barrier = pltpu.get_barrier_semaphore()
    others = [me ^ (1 << bit) for bit in range(levels)]
    others += [lax.rem(me + 1, devices), lax.rem(me + devices - 1, devices)]
    for other in others:
        pl.semaphore_signal(
            barrier, inc=1, device_id=(other,), device_id_type=pl.DeviceIdType.MESH
        )
    pl.semaphore_wait(barrier, len(others))


class Halving:
    def __init__(self, me, order, stages, inbox, send_sems, recv_sems):
        self.me, self.order = me, order
        self.stages, self.inbox = stages, inbox
        self.sems = (send_sems, recv_sems)
        self.copies = []

    def start(self, step):
        bit = self.order[step]
        count = self.stages[step].shape[0] // 2
        mine = (self.me // (1 << bit)) % 2
        self.mine, self.count = mine, count
        self.copies.append(
            send(
                self.stages[step].at[pl.ds((1 - mine) * count, count)],
                self.inbox[step],
                self.sems[0].at[step],
                self.sems[1].at[step],
                self.me ^ (1 << bit),
            )
        )

    def finish(self, step):
        self.copies[step].wait_recv()
        kept = self.stages[step][pl.ds(self.mine * self.count, self.count)]
        total = kept + self.inbox[step][...]
        if step + 1 < len(self.order):
            self.stages[step + 1][...] = total
        return total

    def advance(self):
        step = len(self.copies)
        if step < len(self.order):
            if step:
                self.finish(step - 1)
            self.start(step)


def block_kernel(
    devices,
    scale,
    messages,
    index_row,
    basis,
    w_basis,
    w_rev,
    w_layers,
    cotangent,
    out,
    grad_out,
    layer_out,
    rev_out,
    basis_out,
    *scratch,
):
    levels = devices.bit_length() - 1
    edges, width = messages.shape
    halo = group = edges // 4
    depth = w_layers.shape[0]
    inboxes, scratch = scratch[:levels], scratch[levels:]
    kept, scratch = scratch[: levels - 1], scratch[levels - 1 :]
    (
        parts,
        window,
        arrived,
        returned,
        g_rev,
        gathered,
        tri_weight,
        window_grad,
        rims,
        basis_in,
        basis_sum,
        send_sems,
        recv_sems,
        row_send,
        row_recv,
    ) = scratch
    me = lax.axis_index("edges")
    ahead, behind = lax.rem(me + 1, devices), lax.rem(me + devices - 1, devices)
    bits = (0, levels // 3, 2 * levels // 3, levels - 1)
    greet(me, devices)

    def row_copy(source, target, slot, device):
        return send(source, target, row_send.at[slot], row_recv.at[slot], device)

    halos = [
        row_copy(messages.at[pl.ds(edges - halo, halo)], window.at[pl.ds(0, halo)], 0, ahead),
        row_copy(
            messages.at[pl.ds(0, halo)], window.at[pl.ds(halo + edges, halo)], 1, behind
        ),
    ]

    def exchange(rows, target, first, groups):
        copies = {}
        for k in reversed(groups):
            copies[k] = row_copy(
                rows.at[pl.ds(k * group, group)], target.at[k], first + k, me ^ (1 << bits[k])
            )
        return copies

    def collect(copies, target, groups):
        highs, lows = [], []
        for k in groups:
            onehot = onehot_rows(slot_col[k * group : (k + 1) * group, :], group)
            copies[k].wait_recv()
            ah, al = split(target[k])
            highs.append(dot(onehot, ah).astype(BF16))
            lows.append(dot(onehot, al).astype(BF16))
        return jnp.concatenate(highs, axis=0), jnp.concatenate(lows, axis=0)

    forth = exchange(messages, arrived, 2, range(4))
    slots = basis.shape[1]
    src_row, tgt_row = index_row[:, :slots], index_row[:, slots : 2 * slots]
    src_col, tgt_col = column_of(src_row), column_of(tgt_row)
    slot_col = column_of(index_row[:, 2 * slots :])
    window[halo : halo + edges, :] = messages[...]
    tri_weight[...] = triplet_weight(basis[...], w_basis[...])
    weights = [split(w_layers[layer]) for layer in range(depth)]
    weight_rev = split(w_rev[...])
    for copy in halos:
        copy.wait_recv()
    gathered[...] = pick(onehot_rows(src_col, edges + 2 * halo), window[...])
    agg = pick(onehot_columns(tgt_row, edges), gathered[...] * tri_weight[...])

    def forward(groups):
        start, stop = groups[0] * group, (groups[-1] + 1) * group
        rev = collect(forth, arrived, groups)
        gate, rev_slope = silu_pair(dot3(rev, weight_rev))
        msg = messages[start:stop, :]
        hidden = msg + agg[start:stop, :] + msg * gate
        states, slopes = [], []
        for layer in range(depth):
            state = split(hidden)
            act, slope = silu_pair(dot3(state, weights[layer]))
            hidden = hidden + act
            states.append(state)
            slopes.append(slope)
        out[start:stop, :] = hidden
        return start, stop, rev, gate, rev_slope, states, slopes

    def step_back(grad, slope, weight):
        grad_pre = split(grad * slope)
        return grad_pre, grad + dot3(grad_pre, weight, ((1,), (1,)))

    def leave(done, grad, groups):
        start, stop, _, gate, rev_slope, _, _ = done
        g_rev[start:stop, :] = grad * messages[start:stop, :] * rev_slope
        grad_out[start:stop, :] = grad * (1.0 + gate)
        return exchange(g_rev, returned, 6, groups)

    def joined(first, second):
        return tuple(jnp.concatenate(pair, axis=0) for pair in zip(first, second))

    early, late = range(0, 2), range(2, 4)
    done_a = forward(early)
    grad_a = cotangent[done_a[0] : done_a[1], :]
    pres_a = [None] * depth
    for layer in range(depth - 1, -1, -1):
        pres_a[layer], grad_a = step_back(grad_a, done_a[6][layer], weights[layer])
    back = leave(done_a, grad_a, early)
    done_b = forward(late)
    grad_b = cotangent[done_b[0] : done_b[1], :]

    orders = routes(devices)
    chains = []
    for m in range(depth + 1):
        for r in range(2):
            c = 2 * m + r
            stages = [parts.at[m, r]] + [ref.at[c] for ref in kept]
            inbox = [ref.at[c] for ref in inboxes]
            chains.append(
                Halving(me, orders[r], stages, inbox, send_sems.at[c], recv_sems.at[c])
            )

    def advance(m):
        chains[2 * m].advance()
        chains[2 * m + 1].advance()

    for layer in range(depth - 1, -1, -1):
        pre, grad_b = step_back(grad_b, done_b[6][layer], weights[layer])
        if layer == 0:
            back.update(leave(done_b, grad_b, late))
        state = joined(done_a[5][layer], done_b[5][layer])
        product = dot3(state, joined(pres_a[layer], pre), ((0,), (0,)))
        spread(parts, layer, product * scale)
        for m in range(depth - 1, layer - 1, -1):
            advance(m)
    grad = jnp.concatenate([grad_a, grad_b], axis=0)
    rev = joined(done_a[2], done_b[2])
    spread(parts, depth, dot3(rev, split(g_rev[...]), ((0,), (0,))) * scale)
    advance(depth)
    advance(0)
    grad_prod = pick(onehot_rows(tgt_col, edges), grad)
    basis_sum[0] = dot3(split(basis[...]), split(grad_prod * gathered[...])) * scale
    last = len(chains)
    basis_copies = []

    def basis_advance():
        step = len(basis_copies)
        if step:
            basis_copies[-1].wait_recv()
            basis_sum[step] = basis_sum[step - 1] + basis_in[step - 1]
        if step < levels:
            basis_copies.append(
                send(
                    basis_sum.at[step],
                    basis_in.at[step],
                    send_sems.at[last, step],
                    recv_sems.at[last, step],
                    me ^ (1 << step),
                )
            )

    basis_advance()
    advance(depth)
    window_grad[...] = pick(
        onehot_columns(src_row, edges + 2 * halo), grad_prod * tri_weight[...]
    )
    rim_copies = [
        row_copy(window_grad.at[pl.ds(0, halo)], rims.at[0], 10, behind),
        row_copy(window_grad.at[pl.ds(halo + edges, halo)], rims.at[1], 11, ahead),
    ]
    for m in range(depth - 1, -1, -1):
        advance(m)
    basis_advance()
    grad_out[...] = (
        grad_out[...]
        + window_grad[halo : halo + edges, :]
        + dot3(collect(back, returned, range(4)), weight_rev, ((1,), (1,)))
    )
    advance(depth)
    for step in range(2, levels):
        for m in list(range(depth - 1, -1, -1)) + [depth]:
            advance(m)
        basis_advance()
    rim_copies[0].wait_recv()
    grad_out[edges - halo :, :] = grad_out[edges - halo :, :] + rims[0]
    rim_copies[1].wait_recv()
    grad_out[:halo, :] = grad_out[:halo, :] + rims[1]
    rows, half = parts.shape[3], parts.shape[4]
    for c, chain in enumerate(chains):
        while len(chain.copies) < levels:
            chain.advance()
        total = chain.finish(levels - 1)
        m, r = c // 2, c % 2
        for row in range(rows):
            spot = slice(row * width + r * half, row * width + (r + 1) * half)
            if m < depth:
                layer_out[m : m + 1, spot] = total[0, row : row + 1, :]
            else:
                rev_out[0:1, spot] = total[0, row : row + 1, :]
    basis_advance()
    basis_out[...] = basis_sum[levels]
    for copy in halos + list(forth.values()) + list(back.values()) + rim_copies + basis_copies:
        copy.wait_send()
    for chain in chains:
        for copy in chain.copies:
            copy.wait_send()


def on_device(
    messages,
    rev_slot,
    tri_basis,
    tri_source,
    tri_target,
    tile_block,
    tile_count,
    w_basis,
    w_rev,
    w_layers,
    cotangent,
):
    devices = lax.axis_size("edges")
    levels = devices.bit_length() - 1
    edges, width = messages.shape
    halo = edges // 4
    depth = w_layers.shape[0]
    tiles = tile_block.shape[0]
    slots = tri_source.shape[0]
    scale = float(edges * devices) ** (-0.5)

    live = jnp.arange(tiles, dtype=jnp.int32) < tile_count[0]
    target = tile_block[:, None] * 128 + tri_target.reshape(tiles, 128)
    target = jnp.where(live[:, None], target, -1)
    index_row = jnp.concatenate([tri_source, target.reshape(slots), rev_slot]).reshape(1, -1)

    rows, half, chains = width // devices, width // 2, 2 * (depth + 1)
    sizes = [devices >> (step + 1) for step in range(levels)]
    scratch = [pltpu.VMEM((chains, size, rows, half), F32) for size in sizes]
    scratch += [pltpu.VMEM((chains, size, rows, half), F32) for size in sizes[:-1]]
    scratch += [
        pltpu.VMEM((depth + 1, 2, devices, rows, half), F32),
        pltpu.VMEM((edges + 2 * halo, width), F32),
        pltpu.VMEM((4, halo, width), F32),
        pltpu.VMEM((4, halo, width), F32),
        pltpu.VMEM((edges, width), F32),
        pltpu.VMEM((slots, width), F32),
        pltpu.VMEM((slots, width), F32),
        pltpu.VMEM((edges + 2 * halo, width), F32),
        pltpu.VMEM((2, halo, width), F32),
        pltpu.VMEM((levels,) + w_basis.shape, F32),
        pltpu.VMEM((levels + 1,) + w_basis.shape, F32),
        pltpu.SemaphoreType.DMA((chains + 1, levels)),
        pltpu.SemaphoreType.DMA((chains + 1, levels)),
        pltpu.SemaphoreType.DMA((12,)),
        pltpu.SemaphoreType.DMA((12,)),
    ]
    shapes = [
        (edges, width),
        (edges, width),
        (depth, width * rows),
        (1, width * rows),
        w_basis.shape,
    ]
    specs = [pl.BlockSpec(memory_space=pltpu.VMEM)]
    out, grad_out, layer_share, rev_share, grad_basis = pl.pallas_call(
        lambda *refs: block_kernel(devices, scale, *refs),
        out_shape=[jax.ShapeDtypeStruct(shape, F32) for shape in shapes],
        in_specs=specs * 7,
        out_specs=specs * 5,
        scratch_shapes=scratch,
        compiler_params=pltpu.CompilerParams(
            vmem_limit_bytes=VMEM_LIMIT, collective_id=0, has_side_effects=True
        ),
        name="block",
    )(
        messages,
        index_row,
        tri_basis,
        w_basis,
        w_rev,
        w_layers,
        cotangent,
    )
    return (out, grad_out, layer_share, rev_share.reshape(-1), grad_basis)


def solution(mesh):
    in_specs = (
        P("edges", None),
        P("edges"),
        P(None, "edges"),
        P("edges"),
        P("edges"),
        P("edges"),
        P("edges"),
        P(),
        P(),
        P(),
        P("edges", None),
    )
    out_specs = (P("edges", None), P("edges", None), P(None, "edges"), P("edges"), P())
    return jax.shard_map(
        on_device, mesh=mesh, in_specs=in_specs, out_specs=out_specs, check_vma=False
    )
```

```python
import jax
import jax.numpy as jnp
from jax import lax
from jax.experimental import pallas as pl
from jax.experimental.pallas import tpu as pltpu
from jax.sharding import PartitionSpec as P

F32 = jnp.float32
BF16 = jnp.bfloat16
VMEM_LIMIT = 56 * 1024 * 1024


def split(value):
    high = value.astype(BF16)
    low = (value - high.astype(F32)).astype(BF16)
    return high, low


def dot(left, right, dims=((1,), (0,))):
    return lax.dot_general(left, right, (dims, ((), ())), preferred_element_type=F32)


def dot3(left, right, dims=((1,), (0,))):
    (lh, ll), (rh, rl) = left, right
    return dot(lh, rh, dims) + dot(lh, rl, dims) + dot(ll, rh, dims)


def pick(onehot, value):
    high, low = split(value)
    return dot(onehot, high) + dot(onehot, low)


def onehot_rows(column, width):
    ids = lax.broadcasted_iota(jnp.int32, (column.shape[0], width), 1)
    return jnp.where(column == ids, 1.0, 0.0).astype(BF16)


def column_of(row):
    return jnp.broadcast_to(row, (8, row.shape[1])).T[:, :1]


def onehot_columns(row, height):
    ids = lax.broadcasted_iota(jnp.int32, (height, row.shape[1]), 0)
    return jnp.where(row == ids, 1.0, 0.0).astype(BF16)


def silu_pair(values):
    sigma = jax.nn.sigmoid(values)
    return values * sigma, sigma * (1.0 + values * (1.0 - sigma))


def triplet_weight(basis, w_basis):
    bh, bl = split(basis)
    wh, wl = split(w_basis)
    return dot(
        jnp.concatenate([bh, bl, bh], axis=0),
        jnp.concatenate([wh, wh, wl], axis=0),
        ((0,), (0,)),
    )


def spread(target, index, value):
    devices, rows, half = target.shape[2:]
    for r, order in enumerate(routes(devices)):
        for shard in range(devices):
            target[index, r, place(shard, order)] = value[
                shard * rows : (shard + 1) * rows, r * half : (r + 1) * half
            ]


def routes(devices):
    levels = devices.bit_length() - 1
    first = list(range(levels))
    second = list(first)
    if levels > 2:
        second[1], second[2] = second[2], second[1]
    return first, second


def place(shard, order):
    spot = 0
    for bit in order:
        spot = 2 * spot + ((shard >> bit) & 1)
    return spot


def send(source, target, send_sem, recv_sem, device):
    copy = pltpu.make_async_remote_copy(
        src_ref=source,
        dst_ref=target,
        send_sem=send_sem,
        recv_sem=recv_sem,
        device_id=(device,),
        device_id_type=pl.DeviceIdType.MESH,
    )
    copy.start()
    return copy


def greet(me, devices):
    levels = devices.bit_length() - 1
    barrier = pltpu.get_barrier_semaphore()
    others = [me ^ (1 << bit) for bit in range(levels)]
    others += [lax.rem(me + 1, devices), lax.rem(me + devices - 1, devices)]
    for other in others:
        pl.semaphore_signal(
            barrier, inc=1, device_id=(other,), device_id_type=pl.DeviceIdType.MESH
        )
    pl.semaphore_wait(barrier, len(others))


class Halving:
    def __init__(self, me, order, stages, inbox, send_sems, recv_sems):
        self.me, self.order = me, order
        self.stages, self.inbox = stages, inbox
        self.sems = (send_sems, recv_sems)
        self.copies = []

    def start(self, step):
        bit = self.order[step]
        count = self.stages[step].shape[0] // 2
        mine = (self.me // (1 << bit)) % 2
        self.mine, self.count = mine, count
        self.copies.append(
            send(
                self.stages[step].at[pl.ds((1 - mine) * count, count)],
                self.inbox[step],
                self.sems[0].at[step],
                self.sems[1].at[step],
                self.me ^ (1 << bit),
            )
        )

    def finish(self, step):
        self.copies[step].wait_recv()
        kept = self.stages[step][pl.ds(self.mine * self.count, self.count)]
        total = kept + self.inbox[step][...]
        if step + 1 < len(self.order):
            self.stages[step + 1][...] = total
        return total

    def advance(self):
        step = len(self.copies)
        if step < len(self.order):
            if step:
                self.finish(step - 1)
            self.start(step)


def block_kernel(
    devices,
    scale,
    messages,
    index_row,
    basis,
    w_basis,
    w_rev,
    w_layers,
    cotangent,
    out,
    grad_out,
    layer_out,
    rev_out,
    basis_out,
    *scratch,
):
    levels = devices.bit_length() - 1
    edges, width = messages.shape
    halo = group = edges // 4
    depth = w_layers.shape[0]
    inboxes, scratch = scratch[:levels], scratch[levels:]
    kept, scratch = scratch[: levels - 1], scratch[levels - 1 :]
    (
        parts,
        window,
        arrived,
        returned,
        g_rev,
        gathered,
        tri_weight,
        window_grad,
        rims,
        basis_in,
        basis_sum,
        send_sems,
        recv_sems,
        row_send,
        row_recv,
    ) = scratch
    me = lax.axis_index("edges")
    ahead, behind = lax.rem(me + 1, devices), lax.rem(me + devices - 1, devices)
    bits = (0, levels // 3, 2 * levels // 3, levels - 1)
    greet(me, devices)

    def row_copy(source, target, slot, device):
        return send(source, target, row_send.at[slot], row_recv.at[slot], device)

    halos = [
        row_copy(messages.at[pl.ds(edges - halo, halo)], window.at[pl.ds(0, halo)], 0, ahead),
        row_copy(
            messages.at[pl.ds(0, halo)], window.at[pl.ds(halo + edges, halo)], 1, behind
        ),
    ]

    def exchange(rows, target, first, groups):
        copies = {}
        for k in reversed(groups):
            copies[k] = row_copy(
                rows.at[pl.ds(k * group, group)], target.at[k], first + k, me ^ (1 << bits[k])
            )
        return copies

    def collect(copies, target, groups):
        highs, lows = [], []
        for k in groups:
            onehot = onehot_rows(slot_col[k * group : (k + 1) * group, :], group)
            copies[k].wait_recv()
            ah, al = split(target[k])
            highs.append(dot(onehot, ah).astype(BF16))
            lows.append(dot(onehot, al).astype(BF16))
        return jnp.concatenate(highs, axis=0), jnp.concatenate(lows, axis=0)

    forth = exchange(messages, arrived, 2, range(4))
    slots = basis.shape[1]
    src_row, tgt_row = index_row[:, :slots], index_row[:, slots : 2 * slots]
    src_col, tgt_col = column_of(src_row), column_of(tgt_row)
    slot_col = column_of(index_row[:, 2 * slots :])
    window[halo : halo + edges, :] = messages[...]
    tri_weight[...] = triplet_weight(basis[...], w_basis[...])
    weights = [split(w_layers[layer]) for layer in range(depth)]
    weight_rev = split(w_rev[...])
    for copy in halos:
        copy.wait_recv()
    gathered[...] = pick(onehot_rows(src_col, edges + 2 * halo), window[...])
    agg = pick(onehot_columns(tgt_row, edges), gathered[...] * tri_weight[...])

    def forward(groups):
        start, stop = groups[0] * group, (groups[-1] + 1) * group
        rev = collect(forth, arrived, groups)
        gate, rev_slope = silu_pair(dot3(rev, weight_rev))
        msg = messages[start:stop, :]
        hidden = msg + agg[start:stop, :] + msg * gate
        states, slopes = [], []
        for layer in range(depth):
            state = split(hidden)
            act, slope = silu_pair(dot3(state, weights[layer]))
            hidden = hidden + act
            states.append(state)
            slopes.append(slope)
        out[start:stop, :] = hidden
        return start, stop, rev, gate, rev_slope, states, slopes

    def step_back(grad, slope, weight):
        grad_pre = split(grad * slope)
        return grad_pre, grad + dot3(grad_pre, weight, ((1,), (1,)))

    def leave(done, grad, groups):
        start, stop, _, gate, rev_slope, _, _ = done
        g_rev[start:stop, :] = grad * messages[start:stop, :] * rev_slope
        grad_out[start:stop, :] = grad * (1.0 + gate)
        return exchange(g_rev, returned, 6, groups)

    def joined(first, second):
        return tuple(jnp.concatenate(pair, axis=0) for pair in zip(first, second))

    early, late = range(0, 2), range(2, 4)
    done_a = forward(early)
    grad_a = cotangent[done_a[0] : done_a[1], :]
    pres_a = [None] * depth
    for layer in range(depth - 1, -1, -1):
        pres_a[layer], grad_a = step_back(grad_a, done_a[6][layer], weights[layer])
    back = leave(done_a, grad_a, early)
    done_b = forward(late)
    grad_b = cotangent[done_b[0] : done_b[1], :]

    orders = routes(devices)
    chains = []
    for m in range(depth + 1):
        for r in range(2):
            c = 2 * m + r
            stages = [parts.at[m, r]] + [ref.at[c] for ref in kept]
            inbox = [ref.at[c] for ref in inboxes]
            chains.append(
                Halving(me, orders[r], stages, inbox, send_sems.at[c], recv_sems.at[c])
            )

    def advance(m):
        chains[2 * m].advance()
        chains[2 * m + 1].advance()

    for layer in range(depth - 1, -1, -1):
        pre, grad_b = step_back(grad_b, done_b[6][layer], weights[layer])
        if layer == 0:
            back.update(leave(done_b, grad_b, late))
        state = joined(done_a[5][layer], done_b[5][layer])
        product = dot3(state, joined(pres_a[layer], pre), ((0,), (0,)))
        spread(parts, layer, product * scale)
        for m in range(depth - 1, layer - 1, -1):
            advance(m)
    grad = jnp.concatenate([grad_a, grad_b], axis=0)
    rev = joined(done_a[2], done_b[2])
    spread(parts, depth, dot3(rev, split(g_rev[...]), ((0,), (0,))) * scale)
    advance(depth)
    advance(0)
    grad_prod = pick(onehot_rows(tgt_col, edges), grad)
    basis_sum[0] = dot3(split(basis[...]), split(grad_prod * gathered[...])) * scale
    last = len(chains)
    basis_copies = []

    def basis_advance():
        step = len(basis_copies)
        if step:
            basis_copies[-1].wait_recv()
            basis_sum[step] = basis_sum[step - 1] + basis_in[step - 1]
        if step < levels:
            basis_copies.append(
                send(
                    basis_sum.at[step],
                    basis_in.at[step],
                    send_sems.at[last, step],
                    recv_sems.at[last, step],
                    me ^ (1 << step),
                )
            )

    basis_advance()
    advance(depth - 1)
    advance(depth)
    window_grad[...] = pick(
        onehot_columns(src_row, edges + 2 * halo), grad_prod * tri_weight[...]
    )
    rim_copies = [
        row_copy(window_grad.at[pl.ds(0, halo)], rims.at[0], 10, behind),
        row_copy(window_grad.at[pl.ds(halo + edges, halo)], rims.at[1], 11, ahead),
    ]
    for m in range(depth - 1, -1, -1):
        advance(m)
    basis_advance()
    for step in range(2, levels):
        if step == levels - 1:
            grad_out[...] = (
                grad_out[...]
                + window_grad[halo : halo + edges, :]
                + dot3(collect(back, returned, range(4)), weight_rev, ((1,), (1,)))
            )
        for m in list(range(depth - 1, -1, -1)) + [depth]:
            advance(m)
        basis_advance()
    rim_copies[0].wait_recv()
    grad_out[edges - halo :, :] = grad_out[edges - halo :, :] + rims[0]
    rim_copies[1].wait_recv()
    grad_out[:halo, :] = grad_out[:halo, :] + rims[1]
    rows, half = parts.shape[3], parts.shape[4]
    for c, chain in enumerate(chains):
        while len(chain.copies) < levels:
            chain.advance()
        total = chain.finish(levels - 1)
        m, r = c // 2, c % 2
        for row in range(rows):
            spot = slice(row * width + r * half, row * width + (r + 1) * half)
            if m < depth:
                layer_out[m : m + 1, spot] = total[0, row : row + 1, :]
            else:
                rev_out[0:1, spot] = total[0, row : row + 1, :]
    basis_advance()
    basis_out[...] = basis_sum[levels]
    for copy in halos + list(forth.values()) + list(back.values()) + rim_copies + basis_copies:
        copy.wait_send()
    for chain in chains:
        for copy in chain.copies:
            copy.wait_send()


def on_device(
    messages,
    rev_slot,
    tri_basis,
    tri_source,
    tri_target,
    tile_block,
    tile_count,
    w_basis,
    w_rev,
    w_layers,
    cotangent,
):
    devices = lax.axis_size("edges")
    levels = devices.bit_length() - 1
    edges, width = messages.shape
    halo = edges // 4
    depth = w_layers.shape[0]
    tiles = tile_block.shape[0]
    slots = tri_source.shape[0]
    scale = float(edges * devices) ** (-0.5)

    live = jnp.arange(tiles, dtype=jnp.int32) < tile_count[0]
    target = tile_block[:, None] * 128 + tri_target.reshape(tiles, 128)
    target = jnp.where(live[:, None], target, -1)
    index_row = jnp.concatenate([tri_source, target.reshape(slots), rev_slot]).reshape(1, -1)

    rows, half, chains = width // devices, width // 2, 2 * (depth + 1)
    sizes = [devices >> (step + 1) for step in range(levels)]
    scratch = [pltpu.VMEM((chains, size, rows, half), F32) for size in sizes]
    scratch += [pltpu.VMEM((chains, size, rows, half), F32) for size in sizes[:-1]]
    scratch += [
        pltpu.VMEM((depth + 1, 2, devices, rows, half), F32),
        pltpu.VMEM((edges + 2 * halo, width), F32),
        pltpu.VMEM((4, halo, width), F32),
        pltpu.VMEM((4, halo, width), F32),
        pltpu.VMEM((edges, width), F32),
        pltpu.VMEM((slots, width), F32),
        pltpu.VMEM((slots, width), F32),
        pltpu.VMEM((edges + 2 * halo, width), F32),
        pltpu.VMEM((2, halo, width), F32),
        pltpu.VMEM((levels,) + w_basis.shape, F32),
        pltpu.VMEM((levels + 1,) + w_basis.shape, F32),
        pltpu.SemaphoreType.DMA((chains + 1, levels)),
        pltpu.SemaphoreType.DMA((chains + 1, levels)),
        pltpu.SemaphoreType.DMA((12,)),
        pltpu.SemaphoreType.DMA((12,)),
    ]
    shapes = [
        (edges, width),
        (edges, width),
        (depth, width * rows),
        (1, width * rows),
        w_basis.shape,
    ]
    specs = [pl.BlockSpec(memory_space=pltpu.VMEM)]
    out, grad_out, layer_share, rev_share, grad_basis = pl.pallas_call(
        lambda *refs: block_kernel(devices, scale, *refs),
        out_shape=[jax.ShapeDtypeStruct(shape, F32) for shape in shapes],
        in_specs=specs * 7,
        out_specs=specs * 5,
        scratch_shapes=scratch,
        compiler_params=pltpu.CompilerParams(
            vmem_limit_bytes=VMEM_LIMIT, collective_id=0, has_side_effects=True
        ),
        name="block",
    )(
        messages,
        index_row,
        tri_basis,
        w_basis,
        w_rev,
        w_layers,
        cotangent,
    )
    return (out, grad_out, layer_share, rev_share.reshape(-1), grad_basis)


def solution(mesh):
    in_specs = (
        P("edges", None),
        P("edges"),
        P(None, "edges"),
        P("edges"),
        P("edges"),
        P("edges"),
        P("edges"),
        P(),
        P(),
        P(),
        P("edges", None),
    )
    out_specs = (P("edges", None), P("edges", None), P(None, "edges"), P("edges"), P())
    return jax.shard_map(
        on_device, mesh=mesh, in_specs=in_specs, out_specs=out_specs, check_vma=False
    )
```
